32 devices in a mesh: row: 4 (over y, core), col: 8 (over z, x).
Axes of the slice: x: 2, y: 2, z: 4, core: 2. Of those that a mesh axis runs over, the one named last changes fastest.
Arguments:
- theta: float32 [32, 256, 256], P('row', None, 'col'), may hold values from -6 to 6
- left_env: float32 [16, 32, 256, 256], P('row', 'col'), as said below
- right_env: float32 [8, 32, 256, 256], P(None, 'col'), as said below
- left_sector: int32 [32], replicated, may hold values from 0 to 15, as said below
- right_sector: int32 [32], P('row'), may hold values from 0 to 7
- term_on: int32 [32, 32], P('row', 'col'), may hold values 0 or 1
- left_size: int32 [16], replicated, may hold values from 1 to 256, 2560 in all
- right_size: int32 [8], replicated, may hold values from 1 to 256, 1280 in all
Outputs:
- new_theta: float32 [32, 256, 256], P('row', None, 'col')
- energy: float32 [], replicated
The draws below stay inside these ranges and needn't reach their ends.
Inputs may be any that keep to these rules, and one draw needn't show every extreme that they name: `left_sector`: left sector s belongs to row s // 4. Block k belongs to row k // 8. The 8 blocks of one row name distinct left sectors; they name either none or exactly 4 sectors belonging to any one row, and the blocks of every row name 4 sectors belonging to one common row. `left_env`: each tile is symmetric in its last two dimensions. `right_env`: each tile is symmetric in its last two dimensions.
All inputs are finite; a program needn't handle non-finite values. No bound on the sum of `term_on` on one device may be relied on, other than what follows from the above.
Results may differ from the reference program's by a relative error of at most 0.0001.
Values sent between devices are 32-bit elements; how exact they have to be, the bound alone decides.
A program may use at most 128 MiB of HBM per device.

```python
import math
import jax
import jax.numpy as jnp
import numpy as np
from jax import lax

P_SIZE = 256
W = 32
BLK_DEV = 8
SR = 8
ITERS = 2
CAP = 4
SL_DEV = 4
SL = 16
K = 32
N_ROW = 4


def symmetric_tiles(key, count):
    shape = (count, W, P_SIZE, P_SIZE)
    base = jax.random.normal(key, shape, jnp.float32)
    return (base + jnp.swapaxes(base, 2, 3)) * 0.5 ** 0.5 * P_SIZE ** (-0.5)


def draw_left_env(key, part):
    return symmetric_tiles(jax.random.fold_in(key, 3), SL)


def draw_right_env(key, part):
    return symmetric_tiles(jax.random.fold_in(key, 5), SR)


def row_shuffle(key_one):
    return jax.random.permutation(key_one, N_ROW)


def sector_shuffle(key_one):
    return jax.random.permutation(key_one, SL_DEV)


def draw_left_sector(key, part):
    groups = BLK_DEV // CAP
    key_home = jax.random.fold_in(key, 11)
    key_common = jax.random.fold_in(key, 12)
    key_pick = jax.random.fold_in(key, 13)
    common = jax.random.randint(key_common, (), 0, N_ROW)
    row_perms = jax.vmap(row_shuffle)(jax.random.split(key_home, N_ROW))
    where_common = jnp.argmax((row_perms == common).astype(jnp.int32), axis=1)
    first_home = row_perms[:, 0]
    positions = jnp.arange(N_ROW)
    swapped = jnp.where(positions[None, :] == 0, common, jnp.where(positions[None, :] == where_common[:, None], first_home[:, None], row_perms))
    home_rows = swapped[:, :groups]
    local_picks = jax.vmap(sector_shuffle)(jax.random.split(key_pick, N_ROW * groups)).reshape(N_ROW, groups, SL_DEV)[:, :, :CAP]
    sector = home_rows[:, :, None] * SL_DEV + local_picks
    return sector.reshape(K).astype(jnp.int32)


def set_ends(array, stream_key, least, largest):
    dims = array.shape
    place = [jax.random.randint(jax.random.fold_in(stream_key, axis), (), 0, dims[axis]) for axis in range(len(dims))]
    array = array.at[tuple(place)].set(least)
    longest = dims.index(max(dims))
    place[longest] = (place[longest] + 1) % dims[longest]
    return array.at[tuple(place)].set(largest)


def block_levels(rng, dims, cuts, low, top_value):
    factor_of = 1.0
    for dim, blocks in cuts:
        draws = jax.random.uniform(jax.random.fold_in(jax.random.fold_in(rng, 6), dim), (blocks,), jnp.float32, low / len(cuts), top_value / len(cuts))
        factor_of = factor_of * jnp.repeat(jnp.exp(draws), dims[dim] // blocks).reshape((-1,) + (1,) * (len(dims) - 1 - dim))
    return factor_of


def split_up(number_of, total, most, slope):
    loads = [(1 << 20) // math.isqrt(grade ** slope) + 1 for grade in range(2, number_of + 1)]
    spare, given = total - most - (number_of - 1), [1] * (number_of - 1)
    while spare > 0:
        candidates = [i for i in range(number_of - 1) if given[i] < most]
        pool, remaining = sum([loads[i] for i in candidates]), spare
        for i in candidates:
            extra = min(most - given[i], max(1, remaining * loads[i] // pool), spare)
            given[i] = given[i] + extra
            spare = spare - extra
    return np.array([most] + given)


def uneven_parts(own_key, number_of, total, reach, skew):
    if number_of == 2:
        one = jax.random.randint(own_key, (), max(1, total - reach), min(reach, total - 1) + 1)
        return jnp.stack([one, total - one])
    tallies = jnp.asarray(split_up(number_of, total, reach, skew), jnp.int32)
    couples = (number_of - 1) // 2
    donor, sink = tallies[1:1 + 2 * couples:2], tallies[2:2 + 2 * couples:2]
    margin = jnp.minimum(donor - 1, reach - sink)
    moved = jax.random.randint(jax.random.fold_in(own_key, 1), (couples,), 0, 1 << 20) % (margin + 1)
    tallies = tallies.at[1:1 + 2 * couples:2].set(donor - moved).at[2:2 + 2 * couples:2].set(sink + moved)
    return tallies[jax.random.permutation(jax.random.fold_in(own_key, 2), number_of)]


def gaussian(rng, dims, width, reach, cuts=(), held_as=jnp.bfloat16):
    values = jax.random.normal(rng, dims, jnp.float32) * width
    if len(cuts) > 0:
        values = block_levels(rng, dims, cuts, -0.22, 0.18) * values
    return jnp.clip(values, min=-reach, max=reach).astype(held_as)


def setup_inputs(seed: int = 0) -> dict:
    arg_keys = jax.random.split(jax.random.key(seed), 9)
    return {
        "theta": gaussian(arg_keys[0], (K, P_SIZE, P_SIZE), 1.0, 6.0, ((0, 4), (2, 8)), jnp.float32),
        "left_env": draw_left_env(jax.random.fold_in(arg_keys[8], 71), 0),
        "right_env": draw_right_env(jax.random.fold_in(arg_keys[8], 71), 0),
        "left_sector": draw_left_sector(jax.random.fold_in(arg_keys[8], 71), 0),
        "right_sector": set_ends(jax.random.randint(arg_keys[4], (K,), 0, SR), jax.random.fold_in(arg_keys[4], 1), 0, SR - 1).astype(jnp.int32),
        "term_on": set_ends((jax.random.randint(arg_keys[5], (K, W), 0, 4) < 3).astype(jnp.int32), jax.random.fold_in(arg_keys[5], 1), 0, 1),
        "left_size": uneven_parts(arg_keys[6], SL, SL * P_SIZE * 5 // 8, P_SIZE, 1).astype(jnp.int32),
        "right_size": uneven_parts(arg_keys[7], SR, SR * P_SIZE * 5 // 8, P_SIZE, 1).astype(jnp.int32),
    }


highest = lax.Precision.HIGHEST

def reference(theta, left_env, right_env, left_sector, right_sector, term_on, left_size, right_size):
    tile_iota = jnp.arange(P_SIZE, dtype=jnp.int32)
    row_live = left_size[left_sector]
    col_live = right_size[right_sector]
    masks = ((tile_iota[None, :, None] < row_live[:, None, None]) & (tile_iota[None, None, :] < col_live[:, None, None])).astype(jnp.float32)
    weights = term_on.astype(jnp.float32)

    def operate(vector):

        def one_block(packed):
            block, left_id, right_id, block_weights = packed
            left_part = left_env[left_id]
            right_part = right_env[right_id]
            middle = jnp.einsum('wia,ab->wib', left_part, block, precision=highest) * block_weights[:, None, None]
            return jnp.einsum('wib,wjb->ij', middle, right_part, precision=highest)
        result = lax.map(one_block, (vector, left_sector, right_sector, weights))
        return result * masks
    start_vec = theta * masks
    image_vec = operate(start_vec)
    norm_sq = jnp.sum(start_vec * start_vec)
    correlation = jnp.sum(start_vec * image_vec)
    inv_norm = 1.0 / jnp.sqrt(norm_sq)
    basis_vec = start_vec * inv_norm
    applied = image_vec * inv_norm
    ritz_value = correlation / norm_sq
    for turn_index in range(ITERS):
        residual = applied - ritz_value * basis_vec
        res_sq = jnp.sum(residual * residual)
        length = jnp.sqrt(res_sq)
        fresh_vec = residual / length
        fresh_applied = operate(fresh_vec)
        curvature = jnp.sum(fresh_vec * fresh_applied)
        half_gap = 0.5 * (ritz_value - curvature)
        root_term = jnp.sqrt(half_gap * half_gap + res_sq)
        lowest = 0.5 * (ritz_value + curvature) - root_term
        first_coef = curvature - lowest
        pair_norm = jnp.sqrt(first_coef * first_coef + res_sq)
        basis_vec = (first_coef * basis_vec - length * fresh_vec) / pair_norm
        applied = (first_coef * applied - length * fresh_applied) / pair_norm
        ritz_value = lowest
    new_theta = basis_vec * jnp.sqrt(jnp.float32(K * P_SIZE * P_SIZE))
    return (new_theta, ritz_value)
```

```python
import functools

import jax
import jax.numpy as jnp
from jax import lax
from jax.experimental import pallas as pl
from jax.experimental.pallas import tpu as pltpu
from jax.sharding import PartitionSpec as P

ITERS = 2
APPLIES = ITERS + 1
ROUNDS = 2 * ITERS + 1
CORES = 2
MESH = pl.DeviceIdType.MESH


def lookup(small_table, index_list):
    slot_hits = index_list[:, None] == jnp.arange(small_table.shape[0], dtype=jnp.int32)[None, :]
    return jnp.sum(jnp.where(slot_hits, small_table[None, :], 0), axis=1)


def pack_symmetric(tiles):
    half = tiles.shape[-1] // 2
    upper = tiles[..., :half, half:]
    first = tiles[..., :half, :half]
    second = tiles[..., half:, half:]
    rows = lax.broadcasted_iota(jnp.int32, (half, half), 0)
    cols = lax.broadcasted_iota(jnp.int32, (half, half), 1)
    both = jnp.where(rows <= cols, first, second)
    diag = jnp.sum(jnp.where(rows == cols, second, 0.0), axis=-2, keepdims=True)
    fill = jnp.zeros(tiles.shape[:-2] + (7, half), tiles.dtype)
    return jnp.concatenate([upper, both, diag, fill], axis=-2)


def split(x):
    high = x.astype(jnp.bfloat16)
    low = (x - high.astype(jnp.float32)).astype(jnp.bfloat16)
    return high, low


def dot3(a_high, a_low, b_high, b_low):
    mul = functools.partial(jnp.dot, preferred_element_type=jnp.float32)
    return mul(a_high, b_high) + (mul(a_high, b_low) + mul(a_low, b_high))


def tile_sum(x):
    cols = x.shape[-1]
    total = jnp.sum(x.reshape(-1, 8, cols), axis=0)
    return sum(total[:, i : i + 128] for i in range(0, cols, 128))


def kernel(
    n_row,
    n_col,
    total_entries,
    left_ref,
    right_ref,
    weight_ref,
    start_ref,
    mask_ref,
    pack_ref,
    env_ref,
    out_ref,
    energy_ref,
    gathered,
    left_high,
    left_low,
    stage,
    right_high,
    right_low,
    full,
    partial,
    from_right,
    from_left,
    basis,
    applied,
    vector,
    row_sums,
    col_sums,
    env_sem,
    own_sem,
    far_sem,
    near_sem,
    pass_sem,
    gather_sem,
    scatter_sem,
    row_sem,
    col_sem,
):
    blocks, thin, size = start_ref.shape
    sectors, terms = pack_ref.shape[:2]
    half = size // 2
    half_blocks = blocks // 2
    steps = n_col // 2
    n_far = n_row // CORES - 1
    me_row = lax.axis_index("row")
    me_col = lax.axis_index("col")

    def col_at(place):
        place = lax.rem(place + 2 * n_col, n_col)
        back = place // (n_col // 2)
        return (1 - back) * (2 * place) + back * (2 * n_col - 1 - 2 * place)

    odd = lax.rem(me_col, 2)
    place = (1 - odd) * (me_col // 2) + odd * (n_col - 1 - me_col // 2)
    right = col_at(place + 1)
    left = col_at(place - 1)

    def remote(src, dst, sems, row, col):
        return pltpu.make_async_remote_copy(
            src_ref=src,
            dst_ref=dst,
            send_sem=sems.at[0],
            recv_sem=sems.at[1],
            device_id=(row, col),
            device_id_type=MESH,
        )

    barrier = pltpu.get_barrier_semaphore()
    for step in range(1, n_row):
        peer = lax.rem(me_row + step, n_row)
        pl.semaphore_signal(barrier, inc=1, device_id=(peer, me_col), device_id_type=MESH)
    for step in range(1, n_col):
        peer = lax.rem(me_col + step, n_col)
        pl.semaphore_signal(barrier, inc=1, device_id=(me_row, peer), device_id_type=MESH)
    pl.semaphore_wait(barrier, n_row + n_col - 2)

    core = lax.rem(me_row, CORES)
    partner = me_row + 1 - 2 * core

    def sector_slot(row, sector):
        return gathered.at[row * sectors + sector]

    far = []
    for step in range(1, n_far + 1):
        target = lax.rem(me_row + CORES * step, n_row)
        for sector in range(sectors):
            copy = remote(
                pack_ref.at[sector],
                sector_slot(me_row, sector),
                far_sem.at[step - 1, sector],
                target,
                me_col,
            )
            copy.start()
            far.append(copy)
    near = remote(
        pack_ref, gathered.at[pl.ds(me_row * sectors, sectors)], near_sem, partner, me_col
    )
    near.start()
    own = pltpu.make_async_copy(
        pack_ref, gathered.at[pl.ds(me_row * sectors, sectors)], own_sem
    )
    own.start()

    def gather_start(turn):
        full[turn, me_col] = vector[...]

    def gather_step(turn, step):
        last = step == steps - 1
        ahead = col_at(place - step)
        behind = col_at(place + step)
        first_part = pl.ds(0, half_blocks if last else blocks)
        second_part = pl.ds(half_blocks, half_blocks) if last else pl.ds(0, blocks)
        clockwise = full.at[turn, ahead, first_part]
        counter = full.at[turn, behind, second_part]
        pair = (
            remote(clockwise, clockwise, gather_sem.at[turn, step, 0], me_row, right),
            remote(counter, counter, gather_sem.at[turn, step, 1], me_row, left),
        )
        for copy in pair:
            copy.start()
        return pair

    def gather(turn, between):
        gather_start(turn)
        sent = []
        for step in range(steps):
            pair = gather_step(turn, step)
            sent.extend(pair)
            if step == 0:
                between()
            for copy in pair:
                copy.wait_recv()
        for copy in sent:
            copy.wait_send()

    def contract(turn):
        def block_step(block, carry):
            v_high, v_low = split(full[turn, :, block].reshape(size, size))
            sector = right_ref[block]
            total = jnp.zeros((size, size), jnp.float32)
            for term in range(terms):
                spot = block * terms + term
                middle = dot3(v_high, v_low, left_high[spot], left_low[spot])
                m_high, m_low = split(middle * weight_ref[block, term])
                total = total + dot3(
                    right_high[sector, term], right_low[sector, term], m_high, m_low
                )
            partial[:, block] = total.reshape(n_col, thin, size)
            return carry

        lax.fori_loop(0, blocks, block_step, 0)

    def scatter(turn):
        sent = []
        for step in range(steps):
            first = step == 0
            part_one = pl.ds(0, half_blocks if first else blocks)
            part_two = pl.ds(half_blocks, half_blocks) if first else pl.ds(0, blocks)
            low = col_at(place - steps + step)
            high = col_at(place + steps - step)
            if step == 1:
                partial[low, pl.ds(0, half_blocks)] += from_right[turn, 0, pl.ds(0, half_blocks)]
                partial[high, pl.ds(half_blocks, half_blocks)] += from_left[
                    turn, 0, pl.ds(half_blocks, half_blocks)
                ]
            elif step > 1:
                partial[low] += from_right[turn, step - 1]
                partial[high] += from_left[turn, step - 1]
            pair = (
                remote(
                    partial.at[low, part_one],
                    from_right.at[turn, step, part_one],
                    scatter_sem.at[turn, step, 0],
                    me_row,
                    left,
                ),
                remote(
                    partial.at[high, part_two],
                    from_left.at[turn, step, part_two],
                    scatter_sem.at[turn, step, 1],
                    me_row,
                    right,
                ),
            )
            for copy in pair:
                copy.start()
            sent.extend(pair)
            for copy in pair:
                copy.wait_recv()
        for copy in sent:
            copy.wait_send()
        result = partial[me_col] + from_right[turn, steps - 1] + from_left[turn, steps - 1]
        return result * mask_ref[...]

    def combine(index, values):
        count = len(values)
        for i, value in enumerate(values):
            row_sums[index, me_row, i] = tile_sum(value)
        copies = []
        for step in range(1, n_row):
            mine = row_sums.at[index, me_row, pl.ds(0, count)]
            peer = lax.rem(me_row + step, n_row)
            copies.append(remote(mine, mine, row_sem.at[index, step - 1], peer, me_col))
        for copy in copies:
            copy.start()
        for copy in copies:
            copy.wait_recv()
        for i in range(count):
            col_sums[index, me_col, i] = sum(row_sums[index, r, i] for r in range(n_row))
        more = []
        for step in range(1, n_col):
            mine = col_sums.at[index, me_col, pl.ds(0, count)]
            peer = lax.rem(me_col + step, n_col)
            more.append(remote(mine, mine, col_sem.at[index, step - 1], me_row, peer))
        for copy in more:
            copy.start()
        for copy in more:
            copy.wait_recv()
        for copy in copies + more:
            copy.wait_send()
        totals = [sum(col_sums[index, c, i] for c in range(n_col)) for i in range(count)]
        return [jnp.sum(total, axis=(0, 1), keepdims=True) for total in totals]

    def load_right():
        count = env_ref.shape[0]
        copies = [
            pltpu.make_async_copy(env_ref.at[i], stage.at[i % 2], env_sem.at[i % 2])
            for i in range(count)
        ]
        copies[0].start()
        for i in range(count):
            if i + 1 < count:
                copies[i + 1].start()
            copies[i].wait()
            for term in range(terms):
                right_high[i, term], right_low[i, term] = split(stage[i % 2, term])

    def load_left():
        forward = []
        for step in range(1, n_far + 1):
            source = lax.rem(me_row - CORES * step + n_row, n_row)
            for sector in range(sectors):
                far[(step - 1) * sectors + sector].wait_recv()
                slot = sector_slot(source, sector)
                copy = remote(slot, slot, pass_sem.at[step - 1, sector], partner, me_col)
                copy.start()
                forward.append(copy)
        own.wait()
        near.wait_recv()
        for copy in forward:
            copy.wait_recv()
        for copy in far + [near] + forward:
            copy.wait_send()

        rows = lax.broadcasted_iota(jnp.int32, (half, half), 0)
        cols = lax.broadcasted_iota(jnp.int32, (half, half), 1)

        def unpack(block, carry):
            sector = left_ref[block]
            for term in range(terms):
                tile = gathered[sector, term]
                spot = block * terms + term
                upper = tile[:half]
                both = tile[half:size]
                flipped = both.T
                first = jnp.where(rows <= cols, both, flipped)
                second = jnp.where(rows > cols, both, flipped)
                second = jnp.where(rows == cols, tile[size : size + 1], second)
                quarters = (
                    (0, 0, first),
                    (0, half, upper),
                    (half, 0, upper.T),
                    (half, half, second),
                )
                for at_row, at_col, quarter in quarters:
                    high, low = split(quarter)
                    left_high[spot, at_row : at_row + half, at_col : at_col + half] = high
                    left_low[spot, at_row : at_row + half, at_col : at_col + half] = low
            return carry

        lax.fori_loop(0, blocks, unpack, 0)

    vector[...] = start_ref[...]
    gather(0, load_right)
    load_left()
    contract(0)
    image = scatter(0)
    start = start_ref[...]
    norm_sq, correlation = combine(0, (start * start, start * image))
    inv_norm = 1.0 / jnp.sqrt(norm_sq)
    basis[...] = start * inv_norm
    applied[...] = image * inv_norm
    ritz = correlation / norm_sq
    for turn in range(1, ITERS + 1):
        vector[...] = applied[...] - ritz * basis[...]
        found = []

        def between():
            found.extend(combine(2 * turn - 1, (vector[...] * vector[...],)))

        gather(turn, between)
        (res_sq,) = found
        length = jnp.sqrt(res_sq)
        contract(turn)
        fresh_applied = scatter(turn) / length
        fresh = vector[...] / length
        (curvature,) = combine(2 * turn, (fresh * fresh_applied,))
        half_gap = 0.5 * (ritz - curvature)
        root_term = jnp.sqrt(half_gap * half_gap + res_sq)
        lowest = 0.5 * (ritz + curvature) - root_term
        first_coef = curvature - lowest
        pair_norm = jnp.sqrt(first_coef * first_coef + res_sq)
        fresh = vector[...] / length
        basis[...] = (first_coef * basis[...] - length * fresh) / pair_norm
        applied[...] = (first_coef * applied[...] - length * fresh_applied) / pair_norm
        ritz = lowest
    out_ref[...] = basis[...] * jnp.sqrt(jnp.float32(total_entries))
    energy_ref[...] = jnp.broadcast_to(ritz, energy_ref.shape)


def local(
    n_row, n_col, theta, left_env, right_env, left_sector, right_sector, term_on, left_size, right_size
):
    blocks, size, thin = theta.shape
    sectors, terms = left_env.shape[:2]
    row_index = lax.axis_index("row")
    col_index = lax.axis_index("col")
    own_left = lax.dynamic_slice_in_dim(left_sector, row_index * blocks, blocks)
    rows_live = lookup(left_size, own_left)
    cols_live = lookup(right_size, right_sector)
    col_ids = col_index * thin + jnp.arange(thin, dtype=jnp.int32)
    row_ids = jnp.arange(size, dtype=jnp.int32)
    mask = (
        (col_ids[None, :, None] < cols_live[:, None, None])
        & (row_ids[None, None, :] < rows_live[:, None, None])
    ).astype(jnp.float32)
    start = jnp.swapaxes(theta, 1, 2) * mask
    packed = pack_symmetric(left_env)
    half = size // 2
    steps = n_col // 2
    n_far = n_row // CORES - 1
    f32, bf16 = jnp.float32, jnp.bfloat16
    vmem = pl.BlockSpec(memory_space=pltpu.VMEM)
    smem = pl.BlockSpec(memory_space=pltpu.SMEM)
    anywhere = pl.BlockSpec(memory_space=pl.ANY)
    rights = right_env.shape[0]
    dma = pltpu.SemaphoreType.DMA
    new_theta, energy = pl.pallas_call(
        functools.partial(kernel, n_row, n_col, n_row * blocks * size * size),
        out_shape=(
            jax.ShapeDtypeStruct((blocks, thin, size), f32),
            jax.ShapeDtypeStruct((8, 128), f32),
        ),
        in_specs=[smem, smem, smem, vmem, vmem, anywhere, anywhere],
        out_specs=(vmem, vmem),
        scratch_shapes=[
            pltpu.VMEM((n_row * sectors, terms) + packed.shape[2:], f32),
            pltpu.VMEM((blocks * terms, size, size), bf16),
            pltpu.VMEM((blocks * terms, size, size), bf16),
            pltpu.VMEM((2, terms, size, size), f32),
            pltpu.VMEM((rights, terms, size, size), bf16),
            pltpu.VMEM((rights, terms, size, size), bf16),
            pltpu.VMEM((APPLIES, n_col, blocks, thin, size), f32),
            pltpu.VMEM((n_col, blocks, thin, size), f32),
            pltpu.VMEM((APPLIES, steps, blocks, thin, size), f32),
            pltpu.VMEM((APPLIES, steps, blocks, thin, size), f32),
            pltpu.VMEM((blocks, thin, size), f32),
            pltpu.VMEM((blocks, thin, size), f32),
            pltpu.VMEM((blocks, thin, size), f32),
            pltpu.VMEM((ROUNDS, n_row, 2, 8, 128), f32),
            pltpu.VMEM((ROUNDS, n_col, 2, 8, 128), f32),
            dma((2,)),
            dma,
            dma((n_far, sectors, 2)),
            dma((2,)),
            dma((n_far, sectors, 2)),
            dma((APPLIES, steps, 2, 2)),
            dma((APPLIES, steps, 2, 2)),
            dma((ROUNDS, n_row - 1, 2)),
            dma((ROUNDS, n_col - 1, 2)),
        ],
        compiler_params=pltpu.CompilerParams(
            collective_id=0, has_side_effects=True, vmem_limit_bytes=60 * 2**20
        ),
    )(own_left, right_sector, term_on.astype(f32), start, mask, packed, right_env)
    return jnp.swapaxes(new_theta, 1, 2), energy[0, 0]


def solution(mesh):
    placed = (
        P("row", None, "col"),
        P("row", "col", None, None),
        P(None, "col", None, None),
        P(),
        P("row"),
        P("row", "col"),
        P(),
        P(),
    )
    return jax.shard_map(
        functools.partial(local, mesh.shape["row"], mesh.shape["col"]),
        mesh=mesh,
        in_specs=placed,
        out_specs=(P("row", None, "col"), P()),
        check_vma=False,
    )
```

```python
import functools

import jax
import jax.numpy as jnp
from jax import lax
from jax.experimental import pallas as pl
from jax.experimental.pallas import tpu as pltpu
from jax.sharding import PartitionSpec as P

ITERS = 2
APPLIES = ITERS + 1
ROUNDS = 2 * ITERS + 1
CORES = 2
GROUPS = 2
MESH = pl.DeviceIdType.MESH


def lookup(small_table, index_list):
    slot_hits = index_list[:, None] == jnp.arange(small_table.shape[0], dtype=jnp.int32)[None, :]
    return jnp.sum(jnp.where(slot_hits, small_table[None, :], 0), axis=1)


def pack_symmetric(tiles):
    half = tiles.shape[-1] // 2
    upper = tiles[..., :half, half:]
    first = tiles[..., :half, :half]
    second = tiles[..., half:, half:]
    rows = lax.broadcasted_iota(jnp.int32, (half, half), 0)
    cols = lax.broadcasted_iota(jnp.int32, (half, half), 1)
    both = jnp.where(rows <= cols, first, second)
    diag = jnp.sum(jnp.where(rows == cols, second, 0.0), axis=-2, keepdims=True)
    fill = jnp.zeros(tiles.shape[:-2] + (7, half), tiles.dtype)
    return jnp.concatenate([upper, both, diag, fill], axis=-2)


def split(x):
    high = x.astype(jnp.bfloat16)
    low = (x - high.astype(jnp.float32)).astype(jnp.bfloat16)
    return high, low


def tile_sum(x):
    cols = x.shape[-1]
    total = jnp.sum(x.reshape(-1, 8, cols), axis=0)
    return sum(total[:, i : i + 128] for i in range(0, cols, 128))


def kernel(
    n_row,
    n_col,
    total_entries,
    left_ref,
    right_ref,
    weight_ref,
    start_ref,
    mask_ref,
    pack_ref,
    env_ref,
    out_ref,
    energy_ref,
    gathered,
    left_parts,
    stage,
    right_parts,
    full,
    partial,
    from_right,
    from_left,
    basis,
    applied,
    vector,
    curve,
    row_sums,
    col_sums,
    env_sem,
    own_sem,
    far_sem,
    near_sem,
    pass_sem,
    gather_sem,
    scatter_sem,
    row_sem,
    col_sem,
):
    blocks, thin, size = start_ref.shape
    terms, sectors = pack_ref.shape[:2]
    half = size // 2
    group_blocks = blocks // GROUPS
    half_blocks = group_blocks // 2
    steps = n_col // 2
    n_far = n_row // CORES - 1
    me_row = lax.axis_index("row")
    me_col = lax.axis_index("col")

    def col_at(place):
        place = lax.rem(place + 2 * n_col, n_col)
        back = place // (n_col // 2)
        return (1 - back) * (2 * place) + back * (2 * n_col - 1 - 2 * place)

    odd = lax.rem(me_col, 2)
    place = (1 - odd) * (me_col // 2) + odd * (n_col - 1 - me_col // 2)
    right = col_at(place + 1)
    left = col_at(place - 1)

    def remote(src, dst, sems, row, col):
        return pltpu.make_async_remote_copy(
            src_ref=src,
            dst_ref=dst,
            send_sem=sems.at[0],
            recv_sem=sems.at[1],
            device_id=(row, col),
            device_id_type=MESH,
        )

    barrier = pltpu.get_barrier_semaphore()
    for step in range(1, n_row):
        peer = lax.rem(me_row + step, n_row)
        pl.semaphore_signal(barrier, inc=1, device_id=(peer, me_col), device_id_type=MESH)
    for step in range(1, n_col):
        peer = lax.rem(me_col + step, n_col)
        pl.semaphore_signal(barrier, inc=1, device_id=(me_row, peer), device_id_type=MESH)
    pl.semaphore_wait(barrier, n_row + n_col - 2)

    core = lax.rem(me_row, CORES)
    partner = me_row + 1 - 2 * core

    def sector_slots(term, row):
        return gathered[term].at[pl.ds(row * sectors, sectors)]

    far, near, own = [], [], []
    for term in range(terms):
        for step in range(1, n_far + 1):
            copy = remote(
                pack_ref.at[term],
                sector_slots(term, me_row),
                far_sem.at[term, step - 1],
                lax.rem(me_row + CORES * step, n_row),
                me_col,
            )
            copy.start()
            far.append(copy)
    for term in range(terms):
        here = sector_slots(term, me_row)
        near.append(remote(pack_ref.at[term], here, near_sem.at[term], partner, me_col))
        own.append(pltpu.make_async_copy(pack_ref.at[term], here, own_sem.at[term]))
        near[term].start()
        own[term].start()

    def gather(turn, group):
        first = group * group_blocks
        span = pl.ds(first, group_blocks)
        full[turn, me_col, span] = vector[span]
        sent, pair = [], ()
        for step in range(steps):
            for copy in pair:
                copy.wait_recv()
            last = step == steps - 1
            part_one = pl.ds(first, half_blocks) if last else span
            part_two = pl.ds(first + half_blocks, half_blocks) if last else span
            one = full.at[turn, col_at(place - step), part_one]
            two = full.at[turn, col_at(place + step), part_two]
            sems = gather_sem.at[turn, group, step]
            pair = (
                remote(one, one, sems.at[0], me_row, right),
                remote(two, two, sems.at[1], me_row, left),
            )
            for copy in pair:
                copy.start()
            sent.extend(pair)
            yield
        for copy in pair:
            copy.wait_recv()
        for copy in sent:
            copy.wait_send()

    def contract(turn, first, count, term_from, term_to, mode, length=None):
        def block_step(index, carry):
            block = first + index
            vec = full[turn, :, block].reshape(size, size)
            v_high, v_low = split(vec)
            left_side = jnp.concatenate([v_high, v_high, v_low], axis=1)
            middle = jnp.dot(
                left_side,
                left_parts[block, :, term_from * size : term_to * size],
                preferred_element_type=jnp.float32,
            )
            stack = []
            for term in range(term_from, term_to):
                at = (term - term_from) * size
                high, low = split(middle[:, at : at + size] * weight_ref[block, term])
                stack += [high, low, high]
            total = jnp.dot(
                right_parts[right_ref[block], :, 3 * term_from * size : 3 * term_to * size],
                jnp.concatenate(stack, axis=0),
                preferred_element_type=jnp.float32,
            )
            if mode == "product":
                curve[...] += tile_sum(((vec / length) * (total / length))[None])
            else:
                total = total.reshape(n_col, thin, size)
                if mode == "add":
                    total = total + partial[:, block]
                partial[:, block] = total
            return carry

        lax.fori_loop(0, count, block_step, 0)

    def scatter(turn, group):
        first = group * group_blocks
        span = pl.ds(first, group_blocks)
        part_one = pl.ds(first, half_blocks)
        part_two = pl.ds(first + half_blocks, half_blocks)
        sent, pair = [], ()
        for step in range(steps):
            for copy in pair:
                copy.wait_recv()
            low = col_at(place - steps + step)
            high = col_at(place + steps - step)
            if step > 0:
                one = part_one if step == 1 else span
                two = part_two if step == 1 else span
                partial[low, one] += from_right[turn, step - 1, one]
                partial[high, two] += from_left[turn, step - 1, two]
            one = part_one if step == 0 else span
            two = part_two if step == 0 else span
            sems = scatter_sem.at[turn, group, step]
            pair = (
                remote(
                    partial.at[low, one], from_right.at[turn, step, one], sems.at[0], me_row, left
                ),
                remote(
                    partial.at[high, two], from_left.at[turn, step, two], sems.at[1], me_row, right
                ),
            )
            for copy in pair:
                copy.start()
            sent.extend(pair)
            yield
        for copy in pair:
            copy.wait_recv()
        for copy in sent:
            copy.wait_send()

    def drain(*flows):
        flows = list(flows)
        while flows:
            for flow in list(flows):
                if next(flow, "end") == "end":
                    flows.remove(flow)

    def scattered(turn):
        last = steps - 1
        result = partial[me_col] + from_right[turn, last] + from_left[turn, last]
        return result * mask_ref[...]

    def combine(index, values):
        count = len(values)
        for i, value in enumerate(values):
            row_sums[index, me_row, i] = value
        copies = []
        for step in range(1, n_row):
            mine = row_sums.at[index, me_row, pl.ds(0, count)]
            peer = lax.rem(me_row + step, n_row)
            copies.append(remote(mine, mine, row_sem.at[index, step - 1], peer, me_col))
        for copy in copies:
            copy.start()
        for copy in copies:
            copy.wait_recv()
        for i in range(count):
            col_sums[index, me_col, i] = sum(row_sums[index, r, i] for r in range(n_row))
        more = []
        for step in range(1, n_col):
            mine = col_sums.at[index, me_col, pl.ds(0, count)]
            peer = lax.rem(me_col + step, n_col)
            more.append(remote(mine, mine, col_sem.at[index, step - 1], me_row, peer))
        for copy in more:
            copy.start()
        for copy in more:
            copy.wait_recv()
        for copy in copies + more:
            copy.wait_send()
        totals = [sum(col_sums[index, c, i] for c in range(n_col)) for i in range(count)]
        return [jnp.sum(total, axis=(0, 1), keepdims=True) for total in totals]

    def load_right():
        count = env_ref.shape[0]
        copies = [
            pltpu.make_async_copy(env_ref.at[i], stage.at[i % 2], env_sem.at[i % 2])
            for i in range(count)
        ]
        copies[0].start()
        for i in range(count):
            if i + 1 < count:
                copies[i + 1].start()
            copies[i].wait()
            for term in range(terms):
                high, low = split(stage[i % 2, term])
                for part, value in enumerate((high, high, low)):
                    at = (3 * term + part) * size
                    right_parts[i, :, at : at + size] = value

    forward = []

    def pass_left(term):
        for step in range(1, n_far + 1):
            source = lax.rem(me_row - CORES * step + n_row, n_row)
            far[term * n_far + step - 1].wait_recv()
            slots = sector_slots(term, source)
            copy = remote(slots, slots, pass_sem.at[term, step - 1], partner, me_col)
            copy.start()
            forward.append(copy)

    def load_left(term):
        own[term].wait()
        near[term].wait_recv()
        for copy in forward[term * n_far : (term + 1) * n_far]:
            copy.wait_recv()
        rows = lax.broadcasted_iota(jnp.int32, (half, half), 0)
        cols = lax.broadcasted_iota(jnp.int32, (half, half), 1)

        def unpack(block, carry):
            tile = gathered[term][left_ref[block]]
            upper = tile[:half]
            both = tile[half:size]
            flipped = both.T
            first = jnp.where(rows <= cols, both, flipped)
            second = jnp.where(rows > cols, both, flipped)
            second = jnp.where(rows == cols, tile[size : size + 1], second)
            quarters = (
                (0, 0, first),
                (0, half, upper),
                (half, 0, upper.T),
                (half, half, second),
            )
            for at_row, at_col, quarter in quarters:
                at = term * size + at_col
                high, low = split(quarter)
                for part, value in enumerate((high, low, high)):
                    top = part * size + at_row
                    left_parts[block, top : top + half, at : at + half] = value
            return carry

        lax.fori_loop(0, blocks, unpack, 0)

    vector[...] = start_ref[...]
    flows = [gather(0, group) for group in range(GROUPS)]
    for flow in flows:
        next(flow)
    load_right()
    drain(*flows)
    mid_term = terms // 2
    for term in range(mid_term):
        pass_left(term)
        load_left(term)
    for term in range(mid_term, terms):
        if term == mid_term:
            contract(0, 0, blocks, 0, mid_term, "set")
        pass_left(term)
        load_left(term)
    one, two = scatter(0, 0), scatter(0, 1)
    contract(0, 0, group_blocks, mid_term, terms, "add")
    next(one)
    contract(0, group_blocks, half_blocks, mid_term, terms, "add")
    next(one)
    contract(0, group_blocks + half_blocks, half_blocks, mid_term, terms, "add")
    drain(one, two)
    for copy in far + near + forward:
        copy.wait_send()
    image = scattered(0)
    start = start_ref[...]
    norm_sq, correlation = combine(0, (tile_sum(start * start), tile_sum(start * image)))
    inv_norm = 1.0 / jnp.sqrt(norm_sq)
    basis[...] = start * inv_norm
    applied[...] = image * inv_norm
    ritz = correlation / norm_sq
    for turn in range(1, ITERS + 1):
        vector[...] = applied[...] - ritz * basis[...]
        final = turn == ITERS
        mode = "product" if final else "set"
        one, two = gather(turn, 0), gather(turn, 1)
        next(one)
        (res_sq,) = combine(2 * turn - 1, (tile_sum(vector[...] * vector[...]),))
        length = jnp.sqrt(res_sq)
        for _ in range(steps - 1):
            next(one)
        next(two)
        drain(one)
        if final:
            curve[...] = jnp.zeros_like(curve)
        contract(turn, 0, half_blocks, 0, terms, mode, length)
        next(two)
        contract(turn, half_blocks, half_blocks, 0, terms, mode, length)
        next(two)
        if not final:
            back_one, back_two = scatter(turn, 0), scatter(turn, 1)
            next(back_one)
        drain(two)
        contract(turn, group_blocks, half_blocks, 0, terms, mode, length)
        if not final:
            next(back_one)
        contract(turn, group_blocks + half_blocks, half_blocks, 0, terms, mode, length)
        fresh = vector[...] / length
        if final:
            (curvature,) = combine(2 * turn, (curve[...],))
        else:
            drain(back_one, back_two)
            fresh_applied = scattered(turn) / length
            (curvature,) = combine(2 * turn, (tile_sum(fresh * fresh_applied),))
        half_gap = 0.5 * (ritz - curvature)
        root_term = jnp.sqrt(half_gap * half_gap + res_sq)
        lowest = 0.5 * (ritz + curvature) - root_term
        first_coef = curvature - lowest
        pair_norm = jnp.sqrt(first_coef * first_coef + res_sq)
        basis[...] = (first_coef * basis[...] - length * fresh) / pair_norm
        if not final:
            applied[...] = (first_coef * applied[...] - length * fresh_applied) / pair_norm
        ritz = lowest
    out_ref[...] = basis[...] * jnp.sqrt(jnp.float32(total_entries))
    energy_ref[...] = jnp.broadcast_to(ritz, energy_ref.shape)


def local(
    n_row, n_col, theta, left_env, right_env, left_sector, right_sector, term_on, left_size, right_size
):
    blocks, size, thin = theta.shape
    sectors, terms = left_env.shape[:2]
    row_index = lax.axis_index("row")
    col_index = lax.axis_index("col")
    own_left = lax.dynamic_slice_in_dim(left_sector, row_index * blocks, blocks)
    rows_live = lookup(left_size, own_left)
    cols_live = lookup(right_size, right_sector)
    col_ids = col_index * thin + jnp.arange(thin, dtype=jnp.int32)
    row_ids = jnp.arange(size, dtype=jnp.int32)
    mask = (
        (col_ids[None, :, None] < cols_live[:, None, None])
        & (row_ids[None, None, :] < rows_live[:, None, None])
    ).astype(jnp.float32)
    start = jnp.swapaxes(theta, 1, 2) * mask
    packed = jnp.swapaxes(pack_symmetric(left_env), 0, 1)
    steps = n_col // 2
    n_far = n_row // CORES - 1
    f32, bf16 = jnp.float32, jnp.bfloat16
    vmem = pl.BlockSpec(memory_space=pltpu.VMEM)
    smem = pl.BlockSpec(memory_space=pltpu.SMEM)
    anywhere = pl.BlockSpec(memory_space=pl.ANY)
    rights = right_env.shape[0]
    dma = pltpu.SemaphoreType.DMA
    new_theta, energy = pl.pallas_call(
        functools.partial(kernel, n_row, n_col, n_row * blocks * size * size),
        out_shape=(
            jax.ShapeDtypeStruct((blocks, thin, size), f32),
            jax.ShapeDtypeStruct((8, 128), f32),
        ),
        in_specs=[smem, smem, smem, vmem, vmem, anywhere, anywhere],
        out_specs=(vmem, vmem),
        scratch_shapes=[
            [pltpu.VMEM((n_row * sectors,) + packed.shape[2:], f32) for _ in range(terms)],
            pltpu.VMEM((blocks, 3 * size, terms * size), bf16),
            pltpu.VMEM((2, terms, size, size), f32),
            pltpu.VMEM((rights, size, 3 * terms * size), bf16),
            pltpu.VMEM((APPLIES, n_col, blocks, thin, size), f32),
            pltpu.VMEM((n_col, blocks, thin, size), f32),
            pltpu.VMEM((ITERS, steps, blocks, thin, size), f32),
            pltpu.VMEM((ITERS, steps, blocks, thin, size), f32),
            pltpu.VMEM((blocks, thin, size), f32),
            pltpu.VMEM((blocks, thin, size), f32),
            pltpu.VMEM((blocks, thin, size), f32),
            pltpu.VMEM((8, 128), f32),
            pltpu.VMEM((ROUNDS, n_row, 2, 8, 128), f32),
            pltpu.VMEM((ROUNDS, n_col, 2, 8, 128), f32),
            dma((2,)),
            dma((terms,)),
            dma((terms, n_far, 2)),
            dma((terms, 2)),
            dma((terms, n_far, 2)),
            dma((APPLIES, GROUPS, steps, 2, 2)),
            dma((ITERS, GROUPS, steps, 2, 2)),
            dma((ROUNDS, n_row - 1, 2)),
            dma((ROUNDS, n_col - 1, 2)),
        ],
        compiler_params=pltpu.CompilerParams(
            collective_id=0, has_side_effects=True, vmem_limit_bytes=60 * 2**20
        ),
    )(own_left, right_sector, term_on.astype(f32), start, mask, packed, right_env)
    return jnp.swapaxes(new_theta, 1, 2), energy[0, 0]


def solution(mesh):
    placed = (
        P("row", None, "col"),
        P("row", "col", None, None),
        P(None, "col", None, None),
        P(),
        P("row"),
        P("row", "col"),
        P(),
        P(),
    )
    return jax.shard_map(
        functools.partial(local, mesh.shape["row"], mesh.shape["col"]),
        mesh=mesh,
        in_specs=placed,
        out_specs=(P("row", None, "col"), P()),
        check_vma=False,
    )
```

```python
import functools

import jax
import jax.numpy as jnp
from jax import lax
from jax.experimental import pallas as pl
from jax.experimental.pallas import tpu as pltpu
from jax.sharding import PartitionSpec as P

ITERS = 2
APPLIES = ITERS + 1
ROUNDS = 2 * ITERS
CORES = 2
GROUPS = 2
MESH = pl.DeviceIdType.MESH


def lookup(small_table, index_list):
    slot_hits = index_list[:, None] == jnp.arange(small_table.shape[0], dtype=jnp.int32)[None, :]
    return jnp.sum(jnp.where(slot_hits, small_table[None, :], 0), axis=1)


def pack_symmetric(tiles):
    half = tiles.shape[-1] // 2
    upper = tiles[..., :half, half:]
    first = tiles[..., :half, :half]
    second = tiles[..., half:, half:]
    rows = lax.broadcasted_iota(jnp.int32, (half, half), 0)
    cols = lax.broadcasted_iota(jnp.int32, (half, half), 1)
    both = jnp.where(rows <= cols, first, second)
    diag = jnp.sum(jnp.where(rows == cols, second, 0.0), axis=-2, keepdims=True)
    fill = jnp.zeros(tiles.shape[:-2] + (7, half), tiles.dtype)
    return jnp.concatenate([upper, both, diag, fill], axis=-2)


def split(x):
    high = x.astype(jnp.bfloat16)
    low = (x - high.astype(jnp.float32)).astype(jnp.bfloat16)
    return high, low


def tile_sum(x):
    cols = x.shape[-1]
    total = jnp.sum(x.reshape(-1, 8, cols), axis=0)
    return sum(total[:, i : i + 128] for i in range(0, cols, 128))


def kernel(
    n_row,
    n_col,
    total_entries,
    left_ref,
    right_ref,
    weight_ref,
    start_ref,
    mask_ref,
    pack_ref,
    env_ref,
    out_ref,
    energy_ref,
    gathered,
    left_parts,
    stage,
    right_parts,
    full,
    partial,
    from_right,
    from_left,
    images,
    curve,
    row_sums,
    col_sums,
    env_sem,
    own_sem,
    far_sem,
    near_sem,
    pass_sem,
    gather_sem,
    scatter_sem,
    row_sem,
    col_sem,
):
    blocks, thin, size = start_ref.shape
    terms, sectors = pack_ref.shape[:2]
    half = size // 2
    group_blocks = blocks // GROUPS
    half_blocks = group_blocks // 2
    steps = n_col // 2
    n_far = n_row // CORES - 1
    me_row = lax.axis_index("row")
    me_col = lax.axis_index("col")

    def col_at(place):
        place = lax.rem(place + 2 * n_col, n_col)
        back = place // (n_col // 2)
        return (1 - back) * (2 * place) + back * (2 * n_col - 1 - 2 * place)

    odd = lax.rem(me_col, 2)
    place = (1 - odd) * (me_col // 2) + odd * (n_col - 1 - me_col // 2)
    right = col_at(place + 1)
    left = col_at(place - 1)

    def remote(src, dst, sems, row, col):
        return pltpu.make_async_remote_copy(
            src_ref=src,
            dst_ref=dst,
            send_sem=sems.at[0],
            recv_sem=sems.at[1],
            device_id=(row, col),
            device_id_type=MESH,
        )

    barrier = pltpu.get_barrier_semaphore()
    for step in range(1, n_row):
        peer = lax.rem(me_row + step, n_row)
        pl.semaphore_signal(barrier, inc=1, device_id=(peer, me_col), device_id_type=MESH)
    for step in range(1, n_col):
        peer = lax.rem(me_col + step, n_col)
        pl.semaphore_signal(barrier, inc=1, device_id=(me_row, peer), device_id_type=MESH)
    pl.semaphore_wait(barrier, n_row + n_col - 2)

    core = lax.rem(me_row, CORES)
    partner = me_row + 1 - 2 * core

    def sector_slots(term, row):
        return gathered[term].at[pl.ds(row * sectors, sectors)]

    far, near, own = [], [], []
    for term in range(terms):
        for step in range(1, n_far + 1):
            copy = remote(
                pack_ref.at[term],
                sector_slots(term, me_row),
                far_sem.at[term, step - 1],
                lax.rem(me_row + CORES * step, n_row),
                me_col,
            )
            copy.start()
            far.append(copy)
    for term in range(terms):
        here = sector_slots(term, me_row)
        near.append(remote(pack_ref.at[term], here, near_sem.at[term], partner, me_col))
        own.append(pltpu.make_async_copy(pack_ref.at[term], here, own_sem.at[term]))
        near[term].start()
        own[term].start()

    def gather(turn, group):
        first = group * group_blocks
        span = pl.ds(first, group_blocks)
        full[turn, me_col, span] = images[turn - 1, span] if turn else start_ref[span]
        sent, pair = [], ()
        for step in range(steps):
            for copy in pair:
                copy.wait_recv()
            last = step == steps - 1
            part_one = pl.ds(first, half_blocks) if last else span
            part_two = pl.ds(first + half_blocks, half_blocks) if last else span
            one = full.at[turn, col_at(place - step), part_one]
            two = full.at[turn, col_at(place + step), part_two]
            sems = gather_sem.at[turn, group, step]
            pair = (
                remote(one, one, sems.at[0], me_row, right),
                remote(two, two, sems.at[1], me_row, left),
            )
            for copy in pair:
                copy.start()
            sent.extend(pair)
            yield
        for copy in pair:
            copy.wait_recv()
        for copy in sent:
            copy.wait_send()

    def contract(turn, first, count, term_from, term_to, mode, formula, length=None):
        def block_step(index, carry):
            block = first + index
            vec = formula(*(full[i, :, block].reshape(size, size) for i in range(turn + 1)))
            v_high, v_low = split(vec)
            left_side = jnp.concatenate([v_high, v_high, v_low], axis=1)
            middle = jnp.dot(
                left_side,
                left_parts[block, :, term_from * size : term_to * size],
                preferred_element_type=jnp.float32,
            )
            stack = []
            for term in range(term_from, term_to):
                at = (term - term_from) * size
                high, low = split(middle[:, at : at + size] * weight_ref[block, term])
                stack += [high, low, high]
            total = jnp.dot(
                right_parts[right_ref[block], :, 3 * term_from * size : 3 * term_to * size],
                jnp.concatenate(stack, axis=0),
                preferred_element_type=jnp.float32,
            )
            if mode == "product":
                curve[...] += tile_sum(((vec / length) * (total / length))[None])
            else:
                total = total.reshape(n_col, thin, size)
                if mode == "add":
                    total = total + partial[:, block]
                partial[:, block] = total
            return carry

        lax.fori_loop(0, count, block_step, 0)

    def scatter(turn, group):
        first = group * group_blocks
        span = pl.ds(first, group_blocks)
        part_one = pl.ds(first, half_blocks)
        part_two = pl.ds(first + half_blocks, half_blocks)
        sent, pair = [], ()
        for step in range(steps):
            for copy in pair:
                copy.wait_recv()
            low = col_at(place - steps + step)
            high = col_at(place + steps - step)
            if step > 0:
                one = part_one if step == 1 else span
                two = part_two if step == 1 else span
                partial[low, one] += from_right[turn, step - 1, one]
                partial[high, two] += from_left[turn, step - 1, two]
            one = part_one if step == 0 else span
            two = part_two if step == 0 else span
            sems = scatter_sem.at[turn, group, step]
            pair = (
                remote(
                    partial.at[low, one], from_right.at[turn, step, one], sems.at[0], me_row, left
                ),
                remote(
                    partial.at[high, two], from_left.at[turn, step, two], sems.at[1], me_row, right
                ),
            )
            for copy in pair:
                copy.start()
            sent.extend(pair)
            yield
        for copy in pair:
            copy.wait_recv()
        for copy in sent:
            copy.wait_send()

    def drain(*flows):
        flows = list(flows)
        while flows:
            for flow in list(flows):
                if next(flow, "end") == "end":
                    flows.remove(flow)

    def chain(turn, group):
        yield from scatter(turn, group)
        last = steps - 1
        span = pl.ds(group * group_blocks, group_blocks)
        image = partial[me_col, span] + from_right[turn, last, span] + from_left[turn, last, span]
        images[turn, span] = image * mask_ref[span]
        yield from gather(turn + 1, group)

    def ship(turn, rest):
        one, two = chain(turn, 0), chain(turn, 1)
        next(one)
        rest(0)
        next(one)
        rest(1)
        for _ in range(steps + 1):
            next(one)
            next(two)
        return one, two

    def combine(index, totals, values):
        count = len(values)
        for i, value in enumerate(values):
            row_sums[index, me_row, i] = value
        copies = []
        for step in range(1, n_row):
            mine = row_sums.at[index, me_row, pl.ds(0, count)]
            peer = lax.rem(me_row + step, n_row)
            copies.append(remote(mine, mine, row_sem.at[index, step - 1], peer, me_col))
        for copy in copies:
            copy.start()
        yield
        for copy in copies:
            copy.wait_recv()
        for i in range(count):
            col_sums[index, me_col, i] = sum(row_sums[index, r, i] for r in range(n_row))
        more = []
        for step in range(1, n_col):
            mine = col_sums.at[index, me_col, pl.ds(0, count)]
            peer = lax.rem(me_col + step, n_col)
            more.append(remote(mine, mine, col_sem.at[index, step - 1], me_row, peer))
        for copy in more:
            copy.start()
        yield
        for copy in more:
            copy.wait_recv()
        for copy in copies + more:
            copy.wait_send()
        for i in range(count):
            total = sum(col_sums[index, c, i] for c in range(n_col))
            totals.append(jnp.sum(total, axis=(0, 1), keepdims=True))

    def load_right():
        count = env_ref.shape[0]
        copies = [
            pltpu.make_async_copy(env_ref.at[i], stage.at[i % 2], env_sem.at[i % 2])
            for i in range(count)
        ]
        copies[0].start()
        for i in range(count):
            if i + 1 < count:
                copies[i + 1].start()
            copies[i].wait()
            for term in range(terms):
                high, low = split(stage[i % 2, term])
                for part, value in enumerate((high, high, low)):
                    at = (3 * term + part) * size
                    right_parts[i, :, at : at + size] = value

    forward = []

    def pass_left(term):
        for step in range(1, n_far + 1):
            source = lax.rem(me_row - CORES * step + n_row, n_row)
            far[term * n_far + step - 1].wait_recv()
            slots = sector_slots(term, source)
            copy = remote(slots, slots, pass_sem.at[term, step - 1], partner, me_col)
            copy.start()
            forward.append(copy)

    def load_left(term):
        own[term].wait()
        near[term].wait_recv()
        for copy in forward[term * n_far : (term + 1) * n_far]:
            copy.wait_recv()
        rows = lax.broadcasted_iota(jnp.int32, (half, half), 0)
        cols = lax.broadcasted_iota(jnp.int32, (half, half), 1)

        def unpack(block, carry):
            tile = gathered[term][left_ref[block]]
            upper = tile[:half]
            both = tile[half:size]
            flipped = both.T
            first = jnp.where(rows <= cols, both, flipped)
            second = jnp.where(rows > cols, both, flipped)
            second = jnp.where(rows == cols, tile[size : size + 1], second)
            quarters = (
                (0, 0, first),
                (0, half, upper),
                (half, 0, upper.T),
                (half, half, second),
            )
            for at_row, at_col, quarter in quarters:
                at = term * size + at_col
                high, low = split(quarter)
                for part, value in enumerate((high, low, high)):
                    top = part * size + at_row
                    left_parts[block, top : top + half, at : at + half] = value
            return carry

        lax.fori_loop(0, blocks, unpack, 0)

    def plain(start):
        return start

    flows = [gather(0, group) for group in range(GROUPS)]
    for flow in flows:
        next(flow)
    load_right()
    drain(*flows)
    mid_term = terms // 2
    for term in range(mid_term):
        pass_left(term)
        load_left(term)
    for term in range(mid_term, terms):
        if term == mid_term:
            contract(0, 0, blocks, 0, mid_term, "set", plain)
        pass_left(term)
        load_left(term)
    contract(0, 0, group_blocks, mid_term, terms, "add", plain)

    def second_group(turn, *how):
        def rest(part):
            contract(turn, group_blocks + part * half_blocks, half_blocks, *how)

        return rest

    one, two = ship(0, second_group(0, mid_term, terms, "add", plain))
    start, image = start_ref[...], images[0]
    totals = []
    sums = combine(0, totals, (tile_sum(start * start), tile_sum(start * image)))
    next(sums)
    next(one)
    next(two)
    next(sums)
    drain(one)
    next(two)
    drain(sums)
    for copy in far + near + forward:
        copy.wait_send()
    norm_sq, correlation = totals
    inv_norm = 1.0 / jnp.sqrt(norm_sq)
    ritz = correlation / norm_sq

    def first_residual(start, image):
        return image * inv_norm - ritz * (start * inv_norm)

    residual = first_residual(start_ref[...], images[0])
    totals = []
    sums = combine(1, totals, (tile_sum(residual * residual),))
    next(sums)
    contract(1, 0, half_blocks, 0, terms, "set", first_residual)
    next(two)
    next(sums)
    contract(1, half_blocks, half_blocks, 0, terms, "set", first_residual)
    drain(two, sums)
    (res_sq,) = totals
    length = jnp.sqrt(res_sq)

    one, two = ship(1, second_group(1, 0, terms, "set", first_residual))
    fresh = first_residual(start_ref[...], images[0]) / length
    totals = []
    sums = combine(2, totals, (tile_sum(fresh * (images[1] / length)),))
    next(sums)
    next(one)
    next(two)
    next(sums)
    drain(one)
    next(two)
    drain(sums)
    (curvature,) = totals

    def rotation(ritz, curvature, res_sq):
        half_gap = 0.5 * (ritz - curvature)
        root_term = jnp.sqrt(half_gap * half_gap + res_sq)
        lowest = 0.5 * (ritz + curvature) - root_term
        first_coef = curvature - lowest
        pair_norm = jnp.sqrt(first_coef * first_coef + res_sq)
        return lowest, first_coef, 1.0 / pair_norm

    lowest, first_coef, inv_pair = rotation(ritz, curvature, res_sq)

    def second_basis(start, image):
        return (first_coef * (start * inv_norm) - first_residual(start, image)) * inv_pair

    def second_residual(start, image, next_image):
        applied = (first_coef * (image * inv_norm) - next_image) * inv_pair
        return applied - lowest * second_basis(start, image)

    curve[...] = jnp.zeros_like(curve)
    how = (0, terms, "product", second_residual, length)
    contract(2, 0, half_blocks, *how)
    next(two)
    contract(2, half_blocks, half_blocks, *how)
    drain(two)
    contract(2, group_blocks, group_blocks, *how)
    residual = second_residual(start_ref[...], images[0], images[1])
    totals = []
    drain(combine(3, totals, (tile_sum(residual * residual), curve[...])))
    next_res_sq, product = totals
    scale = length / jnp.sqrt(next_res_sq)
    energy, next_coef, next_inv = rotation(lowest, product * scale * scale, next_res_sq)
    basis = second_basis(start_ref[...], images[0])
    residual = second_residual(start_ref[...], images[0], images[1])
    basis = (next_coef * basis - residual) * next_inv
    out_ref[...] = basis * jnp.sqrt(jnp.float32(total_entries))
    energy_ref[...] = jnp.broadcast_to(energy, energy_ref.shape)


def local(
    n_row, n_col, theta, left_env, right_env, left_sector, right_sector, term_on, left_size, right_size
):
    blocks, size, thin = theta.shape
    sectors, terms = left_env.shape[:2]
    row_index = lax.axis_index("row")
    col_index = lax.axis_index("col")
    own_left = lax.dynamic_slice_in_dim(left_sector, row_index * blocks, blocks)
    rows_live = lookup(left_size, own_left)
    cols_live = lookup(right_size, right_sector)
    col_ids = col_index * thin + jnp.arange(thin, dtype=jnp.int32)
    row_ids = jnp.arange(size, dtype=jnp.int32)
    mask = (
        (col_ids[None, :, None] < cols_live[:, None, None])
        & (row_ids[None, None, :] < rows_live[:, None, None])
    ).astype(jnp.float32)
    start = jnp.swapaxes(theta, 1, 2) * mask
    packed = jnp.swapaxes(pack_symmetric(left_env), 0, 1)
    steps = n_col // 2
    n_far = n_row // CORES - 1
    f32, bf16 = jnp.float32, jnp.bfloat16
    vmem = pl.BlockSpec(memory_space=pltpu.VMEM)
    smem = pl.BlockSpec(memory_space=pltpu.SMEM)
    anywhere = pl.BlockSpec(memory_space=pl.ANY)
    rights = right_env.shape[0]
    dma = pltpu.SemaphoreType.DMA
    new_theta, energy = pl.pallas_call(
        functools.partial(kernel, n_row, n_col, n_row * blocks * size * size),
        out_shape=(
            jax.ShapeDtypeStruct((blocks, thin, size), f32),
            jax.ShapeDtypeStruct((8, 128), f32),
        ),
        in_specs=[smem, smem, smem, vmem, vmem, anywhere, anywhere],
        out_specs=(vmem, vmem),
        scratch_shapes=[
            [pltpu.VMEM((n_row * sectors,) + packed.shape[2:], f32) for _ in range(terms)],
            pltpu.VMEM((blocks, 3 * size, terms * size), bf16),
            pltpu.VMEM((2, terms, size, size), f32),
            pltpu.VMEM((rights, size, 3 * terms * size), bf16),
            pltpu.VMEM((APPLIES, n_col, blocks, thin, size), f32),
            pltpu.VMEM((n_col, blocks, thin, size), f32),
            pltpu.VMEM((ITERS, steps, blocks, thin, size), f32),
            pltpu.VMEM((ITERS, steps, blocks, thin, size), f32),
            pltpu.VMEM((ITERS, blocks, thin, size), f32),
            pltpu.VMEM((8, 128), f32),
            pltpu.VMEM((ROUNDS, n_row, 2, 8, 128), f32),
            pltpu.VMEM((ROUNDS, n_col, 2, 8, 128), f32),
            dma((2,)),
            dma((terms,)),
            dma((terms, n_far, 2)),
            dma((terms, 2)),
            dma((terms, n_far, 2)),
            dma((APPLIES, GROUPS, steps, 2, 2)),
            dma((ITERS, GROUPS, steps, 2, 2)),
            dma((ROUNDS, n_row - 1, 2)),
            dma((ROUNDS, n_col - 1, 2)),
        ],
        compiler_params=pltpu.CompilerParams(
            collective_id=0, has_side_effects=True, vmem_limit_bytes=60 * 2**20
        ),
    )(own_left, right_sector, term_on.astype(f32), start, mask, packed, right_env)
    return jnp.swapaxes(new_theta, 1, 2), energy[0, 0]


def solution(mesh):
    placed = (
        P("row", None, "col"),
        P("row", "col", None, None),
        P(None, "col", None, None),
        P(),
        P("row"),
        P("row", "col"),
        P(),
        P(),
    )
    return jax.shard_map(
        functools.partial(local, mesh.shape["row"], mesh.shape["col"]),
        mesh=mesh,
        in_specs=placed,
        out_specs=(P("row", None, "col"), P()),
        check_vma=False,
    )
```

```python
import functools

import jax
import jax.numpy as jnp
from jax import lax
from jax.experimental import pallas as pl
from jax.experimental.pallas import tpu as pltpu
from jax.sharding import PartitionSpec as P

ITERS = 2
APPLIES = ITERS + 1
ROUNDS = 2 * ITERS
CORES = 2
GROUPS = 2
MESH = pl.DeviceIdType.MESH


def lookup(small_table, index_list):
    slot_hits = index_list[:, None] == jnp.arange(small_table.shape[0], dtype=jnp.int32)[None, :]
    return jnp.sum(jnp.where(slot_hits, small_table[None, :], 0), axis=1)


def pack_symmetric(tiles):
    half = tiles.shape[-1] // 2
    upper = tiles[..., :half, half:]
    first = tiles[..., :half, :half]
    second = tiles[..., half:, half:]
    rows = lax.broadcasted_iota(jnp.int32, (half, half), 0)
    cols = lax.broadcasted_iota(jnp.int32, (half, half), 1)
    both = jnp.where(rows <= cols, first, second)
    diag = jnp.sum(jnp.where(rows == cols, second, 0.0), axis=-2, keepdims=True)
    fill = jnp.zeros(tiles.shape[:-2] + (7, half), tiles.dtype)
    return jnp.concatenate([upper, both, diag, fill], axis=-2)


def split(x):
    high = x.astype(jnp.bfloat16)
    low = (x - high.astype(jnp.float32)).astype(jnp.bfloat16)
    return high, low


def tile_sum(x):
    cols = x.shape[-1]
    total = jnp.sum(x.reshape(-1, 8, cols), axis=0)
    return sum(total[:, i : i + 128] for i in range(0, cols, 128))


def kernel(
    n_row,
    n_col,
    total_entries,
    left_ref,
    right_ref,
    weight_ref,
    start_ref,
    mask_ref,
    pack_ref,
    env_ref,
    out_ref,
    energy_ref,
    gathered,
    left_parts,
    stage,
    right_parts,
    full,
    partial,
    from_right,
    from_left,
    images,
    curve,
    row_sums,
    col_sums,
    env_sem,
    own_sem,
    far_sem,
    near_sem,
    pass_sem,
    gather_sem,
    scatter_sem,
    row_sem,
    col_sem,
):
    blocks, thin, size = start_ref.shape
    terms, sectors = pack_ref.shape[:2]
    half = size // 2
    group_blocks = blocks // GROUPS
    half_blocks = group_blocks // 2
    steps = n_col // 2
    n_far = n_row // CORES - 1
    me_row = lax.axis_index("row")
    me_col = lax.axis_index("col")

    def col_at(place):
        place = lax.rem(place + 2 * n_col, n_col)
        back = place // (n_col // 2)
        return (1 - back) * (2 * place) + back * (2 * n_col - 1 - 2 * place)

    odd = lax.rem(me_col, 2)
    place = (1 - odd) * (me_col // 2) + odd * (n_col - 1 - me_col // 2)
    right = col_at(place + 1)
    left = col_at(place - 1)

    def remote(src, dst, sems, row, col):
        return pltpu.make_async_remote_copy(
            src_ref=src,
            dst_ref=dst,
            send_sem=sems.at[0],
            recv_sem=sems.at[1],
            device_id=(row, col),
            device_id_type=MESH,
        )

    barrier = pltpu.get_barrier_semaphore()
    for step in range(1, n_row):
        peer = lax.rem(me_row + step, n_row)
        pl.semaphore_signal(barrier, inc=1, device_id=(peer, me_col), device_id_type=MESH)
    for step in range(1, n_col):
        peer = lax.rem(me_col + step, n_col)
        pl.semaphore_signal(barrier, inc=1, device_id=(me_row, peer), device_id_type=MESH)
    pl.semaphore_wait(barrier, n_row + n_col - 2)

    core = lax.rem(me_row, CORES)
    partner = me_row + 1 - 2 * core

    def sector_slots(term, row):
        return gathered[term].at[pl.ds(row * sectors, sectors)]

    far, near, own = [], [], []
    for term in range(terms):
        for step in range(1, n_far + 1):
            copy = remote(
                pack_ref.at[term],
                sector_slots(term, me_row),
                far_sem.at[term, step - 1],
                lax.rem(me_row + CORES * step, n_row),
                me_col,
            )
            copy.start()
            far.append(copy)
    for term in range(terms):
        here = sector_slots(term, me_row)
        near.append(remote(pack_ref.at[term], here, near_sem.at[term], partner, me_col))
        own.append(pltpu.make_async_copy(pack_ref.at[term], here, own_sem.at[term]))
        near[term].start()
        own[term].start()

    def gather(turn, group):
        first = group * group_blocks
        span = pl.ds(first, group_blocks)
        full[turn, me_col, span] = images[turn - 1, span] if turn else start_ref[span]
        sent, pair = [], ()
        for step in range(steps):
            for copy in pair:
                copy.wait_recv()
            last = step == steps - 1
            part_one = pl.ds(first, half_blocks) if last else span
            part_two = pl.ds(first + half_blocks, half_blocks) if last else span
            one = full.at[turn, col_at(place - step), part_one]
            two = full.at[turn, col_at(place + step), part_two]
            sems = gather_sem.at[turn, group, step]
            pair = (
                remote(one, one, sems.at[0], me_row, right),
                remote(two, two, sems.at[1], me_row, left),
            )
            for copy in pair:
                copy.start()
            sent.extend(pair)
            yield
        for copy in pair:
            copy.wait_recv()
        for copy in sent:
            copy.wait_send()

    def contract(turn, first, count, term_from, term_to, mode, formula, length=None):
        def block_step(index, carry):
            block = first + index
            vec = formula(*(full[i, :, block].reshape(size, size) for i in range(turn + 1)))
            v_high, v_low = split(vec)
            left_side = jnp.concatenate([v_high, v_high, v_low], axis=1)
            middle = jnp.dot(
                left_side,
                left_parts[block, :, term_from * size : term_to * size],
                preferred_element_type=jnp.float32,
            )
            stack = []
            for term in range(term_from, term_to):
                at = (term - term_from) * size
                high, low = split(middle[:, at : at + size] * weight_ref[block, term].astype(jnp.float32))
                stack += [high, low, high]
            total = jnp.dot(
                right_parts[right_ref[block], :, 3 * term_from * size : 3 * term_to * size],
                jnp.concatenate(stack, axis=0),
                preferred_element_type=jnp.float32,
            )
            if mode == "product":
                curve[...] += tile_sum(((vec / length) * (total / length))[None])
            else:
                total = total.reshape(n_col, thin, size)
                if mode == "add":
                    total = total + partial[:, block]
                partial[:, block] = total
            return carry

        lax.fori_loop(0, count, block_step, 0)

    def scatter(turn, group):
        first = group * group_blocks
        span = pl.ds(first, group_blocks)
        part_one = pl.ds(first, half_blocks)
        part_two = pl.ds(first + half_blocks, half_blocks)
        sent, pair = [], ()
        for step in range(steps):
            for copy in pair:
                copy.wait_recv()
            low = col_at(place - steps + step)
            high = col_at(place + steps - step)
            if step > 0:
                one = part_one if step == 1 else span
                two = part_two if step == 1 else span
                partial[low, one] += from_right[turn, step - 1, one]
                partial[high, two] += from_left[turn, step - 1, two]
            one = part_one if step == 0 else span
            two = part_two if step == 0 else span
            sems = scatter_sem.at[turn, group, step]
            pair = (
                remote(
                    partial.at[low, one], from_right.at[turn, step, one], sems.at[0], me_row, left
                ),
                remote(
                    partial.at[high, two], from_left.at[turn, step, two], sems.at[1], me_row, right
                ),
            )
            for copy in pair:
                copy.start()
            sent.extend(pair)
            yield
        for copy in pair:
            copy.wait_recv()
        for copy in sent:
            copy.wait_send()

    def drain(*flows):
        flows = list(flows)
        while flows:
            for flow in list(flows):
                if next(flow, "end") == "end":
                    flows.remove(flow)

    def chain(turn, group):
        yield from scatter(turn, group)
        last = steps - 1
        span = pl.ds(group * group_blocks, group_blocks)
        image = partial[me_col, span] + from_right[turn, last, span] + from_left[turn, last, span]
        images[turn, span] = image * mask_ref[span]
        yield from gather(turn + 1, group)

    def ship(turn, rest):
        one, two = chain(turn, 0), chain(turn, 1)
        next(one)
        rest(0)
        next(one)
        rest(1)
        for _ in range(steps + 1):
            next(one)
            next(two)
        return one, two

    def combine(index, totals, values):
        count = len(values)
        for i, value in enumerate(values):
            row_sums[index, me_row, i] = value
        copies = []
        for step in range(1, n_row):
            mine = row_sums.at[index, me_row, pl.ds(0, count)]
            peer = lax.rem(me_row + step, n_row)
            copies.append(remote(mine, mine, row_sem.at[index, step - 1], peer, me_col))
        for copy in copies:
            copy.start()
        yield
        for copy in copies:
            copy.wait_recv()
        for i in range(count):
            col_sums[index, me_col, i] = sum(row_sums[index, r, i] for r in range(n_row))
        more = []
        for step in range(1, n_col):
            mine = col_sums.at[index, me_col, pl.ds(0, count)]
            peer = lax.rem(me_col + step, n_col)
            more.append(remote(mine, mine, col_sem.at[index, step - 1], me_row, peer))
        for copy in more:
            copy.start()
        yield
        for copy in more:
            copy.wait_recv()
        for copy in copies + more:
            copy.wait_send()
        for i in range(count):
            total = sum(col_sums[index, c, i] for c in range(n_col))
            totals.append(jnp.sum(total, axis=(0, 1), keepdims=True))

    def load_right():
        count = env_ref.shape[0]
        copies = [
            pltpu.make_async_copy(env_ref.at[i], stage.at[i % 2], env_sem.at[i % 2])
            for i in range(count)
        ]
        copies[0].start()
        for i in range(count):
            if i + 1 < count:
                copies[i + 1].start()
            copies[i].wait()
            for term in range(terms):
                high, low = split(stage[i % 2, term])
                for part, value in enumerate((high, high, low)):
                    at = (3 * term + part) * size
                    right_parts[i, :, at : at + size] = value

    forward = []

    def pass_left(term):
        for step in range(1, n_far + 1):
            source = lax.rem(me_row - CORES * step + n_row, n_row)
            far[term * n_far + step - 1].wait_recv()
            slots = sector_slots(term, source)
            copy = remote(slots, slots, pass_sem.at[term, step - 1], partner, me_col)
            copy.start()
            forward.append(copy)

    def load_left(term):
        own[term].wait()
        near[term].wait_recv()
        for copy in forward[term * n_far : (term + 1) * n_far]:
            copy.wait_recv()
        rows = lax.broadcasted_iota(jnp.int32, (half, half), 0)
        cols = lax.broadcasted_iota(jnp.int32, (half, half), 1)

        def unpack(block, carry):
            tile = gathered[term][left_ref[block]]
            upper = tile[:half]
            both = tile[half:size]
            flipped = both.T
            first = jnp.where(rows <= cols, both, flipped)
            second = jnp.where(rows > cols, both, flipped)
            second = jnp.where(rows == cols, tile[size : size + 1], second)
            quarters = (
                (0, 0, first),
                (0, half, upper),
                (half, 0, upper.T),
                (half, half, second),
            )
            for at_row, at_col, quarter in quarters:
                at = term * size + at_col
                high, low = split(quarter)
                for part, value in enumerate((high, low, high)):
                    top = part * size + at_row
                    left_parts[block, top : top + half, at : at + half] = value
            return carry

        lax.fori_loop(0, blocks, unpack, 0)

    def plain(start):
        return start

    flows = [gather(0, group) for group in range(GROUPS)]
    for flow in flows:
        next(flow)
    load_right()
    drain(*flows)
    mid_term = terms - 1
    for term in range(mid_term):
        pass_left(term)
        load_left(term)
    for term in range(mid_term, terms):
        if term == mid_term:
            contract(0, 0, blocks, 0, mid_term, "set", plain)
        pass_left(term)
        load_left(term)
    contract(0, 0, group_blocks, mid_term, terms, "add", plain)

    def second_group(turn, *how):
        def rest(part):
            contract(turn, group_blocks + part * half_blocks, half_blocks, *how)

        return rest

    one, two = ship(0, second_group(0, mid_term, terms, "add", plain))
    start, image = start_ref[...], images[0]
    totals = []
    sums = combine(0, totals, (tile_sum(start * start), tile_sum(start * image)))
    next(sums)
    next(one)
    next(two)
    next(sums)
    drain(one)
    next(two)
    drain(sums)
    for copy in far + near + forward:
        copy.wait_send()
    norm_sq, correlation = totals
    inv_norm = 1.0 / jnp.sqrt(norm_sq)
    ritz = correlation / norm_sq

    def first_residual(start, image):
        return image * inv_norm - ritz * (start * inv_norm)

    residual = first_residual(start_ref[...], images[0])
    totals = []
    sums = combine(1, totals, (tile_sum(residual * residual),))
    next(sums)
    contract(1, 0, half_blocks, 0, terms, "set", first_residual)
    next(two)
    next(sums)
    contract(1, half_blocks, half_blocks, 0, terms, "set", first_residual)
    drain(two, sums)
    (res_sq,) = totals
    length = jnp.sqrt(res_sq)

    one, two = ship(1, second_group(1, 0, terms, "set", first_residual))
    fresh = first_residual(start_ref[...], images[0]) / length
    totals = []
    sums = combine(2, totals, (tile_sum(fresh * (images[1] / length)),))
    next(sums)
    next(one)
    next(two)
    next(sums)
    drain(one)
    next(two)
    drain(sums)
    (curvature,) = totals

    def rotation(ritz, curvature, res_sq):
        half_gap = 0.5 * (ritz - curvature)
        root_term = jnp.sqrt(half_gap * half_gap + res_sq)
        lowest = 0.5 * (ritz + curvature) - root_term
        first_coef = curvature - lowest
        pair_norm = jnp.sqrt(first_coef * first_coef + res_sq)
        return lowest, first_coef, 1.0 / pair_norm

    lowest, first_coef, inv_pair = rotation(ritz, curvature, res_sq)

    def second_basis(start, image):
        return (first_coef * (start * inv_norm) - first_residual(start, image)) * inv_pair

    def second_residual(start, image, next_image):
        applied = (first_coef * (image * inv_norm) - next_image) * inv_pair
        return applied - lowest * second_basis(start, image)

    curve[...] = jnp.zeros_like(curve)
    how = (0, terms, "product", second_residual, length)
    contract(2, 0, half_blocks, *how)
    next(two)
    contract(2, half_blocks, half_blocks, *how)
    drain(two)
    contract(2, group_blocks, group_blocks, *how)
    residual = second_residual(start_ref[...], images[0], images[1])
    totals = []
    drain(combine(3, totals, (tile_sum(residual * residual), curve[...])))
    next_res_sq, product = totals
    scale = length / jnp.sqrt(next_res_sq)
    energy, next_coef, next_inv = rotation(lowest, product * scale * scale, next_res_sq)
    basis = second_basis(start_ref[...], images[0])
    residual = second_residual(start_ref[...], images[0], images[1])
    basis = (next_coef * basis - residual) * next_inv
    out_ref[...] = basis * jnp.sqrt(jnp.float32(total_entries))
    energy_ref[...] = energy


def local(
    n_row, n_col, theta, left_env, right_env, left_sector, right_sector, term_on, left_size, right_size
):
    blocks, size, thin = theta.shape
    sectors, terms = left_env.shape[:2]
    row_index = lax.axis_index("row")
    col_index = lax.axis_index("col")
    own_left = lax.dynamic_slice_in_dim(left_sector, row_index * blocks, blocks)
    rows_live = lookup(left_size, own_left)
    cols_live = lookup(right_size, right_sector)
    col_ids = col_index * thin + jnp.arange(thin, dtype=jnp.int32)
    row_ids = jnp.arange(size, dtype=jnp.int32)
    mask = (
        (col_ids[None, :, None] < cols_live[:, None, None])
        & (row_ids[None, None, :] < rows_live[:, None, None])
    ).astype(jnp.float32)
    start = jnp.swapaxes(theta, 1, 2) * mask
    packed = jnp.swapaxes(pack_symmetric(left_env), 0, 1)
    steps = n_col // 2
    n_far = n_row // CORES - 1
    f32, bf16 = jnp.float32, jnp.bfloat16
    vmem = pl.BlockSpec(memory_space=pltpu.VMEM)
    smem = pl.BlockSpec(memory_space=pltpu.SMEM)
    anywhere = pl.BlockSpec(memory_space=pl.ANY)
    rights = right_env.shape[0]
    dma = pltpu.SemaphoreType.DMA
    new_theta, energy = pl.pallas_call(
        functools.partial(kernel, n_row, n_col, n_row * blocks * size * size),
        out_shape=(
            jax.ShapeDtypeStruct((blocks, thin, size), f32),
            jax.ShapeDtypeStruct((1, 1), f32),
        ),
        in_specs=[smem, smem, smem, vmem, vmem, anywhere, anywhere],
        out_specs=(vmem, vmem),
        scratch_shapes=[
            [pltpu.VMEM((n_row * sectors,) + packed.shape[2:], f32) for _ in range(terms)],
            pltpu.VMEM((blocks, 3 * size, terms * size), bf16),
            pltpu.VMEM((2, terms, size, size), f32),
            pltpu.VMEM((rights, size, 3 * terms * size), bf16),
            pltpu.VMEM((APPLIES, n_col, blocks, thin, size), f32),
            pltpu.VMEM((n_col, blocks, thin, size), f32),
            pltpu.VMEM((ITERS, steps, blocks, thin, size), f32),
            pltpu.VMEM((ITERS, steps, blocks, thin, size), f32),
            pltpu.VMEM((ITERS, blocks, thin, size), f32),
            pltpu.VMEM((8, 128), f32),
            pltpu.VMEM((ROUNDS, n_row, 2, 8, 128), f32),
            pltpu.VMEM((ROUNDS, n_col, 2, 8, 128), f32),
            dma((2,)),
            dma((terms,)),
            dma((terms, n_far, 2)),
            dma((terms, 2)),
            dma((terms, n_far, 2)),
            dma((APPLIES, GROUPS, steps, 2, 2)),
            dma((ITERS, GROUPS, steps, 2, 2)),
            dma((ROUNDS, n_row - 1, 2)),
            dma((ROUNDS, n_col - 1, 2)),
        ],
        compiler_params=pltpu.CompilerParams(
            collective_id=0, has_side_effects=True, vmem_limit_bytes=60 * 2**20
        ),
    )(own_left, right_sector, term_on, start, mask, packed, right_env)
    return jnp.swapaxes(new_theta, 1, 2), energy.reshape(())


def solution(mesh):
    placed = (
        P("row", None, "col"),
        P("row", "col", None, None),
        P(None, "col", None, None),
        P(),
        P("row"),
        P("row", "col"),
        P(),
        P(),
    )
    return jax.shard_map(
        functools.partial(local, mesh.shape["row"], mesh.shape["col"]),
        mesh=mesh,
        in_specs=placed,
        out_specs=(P("row", None, "col"), P()),
        check_vma=False,
    )
```
